128 devices in a mesh: rows: 4 (over z_lo, core), cols: 32 (over y, x, z_hi).
Axes of the slice: x: 4, y: 4, z: 4 (z_hi: 2, z_lo: 2; z = z_hi * 2 + z_lo), core: 2. Of those that a mesh axis runs over, the one named last changes fastest.
Arguments:
- pair_integrals: float32 [4096, 16384], P('rows', 'cols'), may hold values from -6 to 6
- left_factor: float32 [4096, 1024], P('rows', 'cols'), may hold values from -0.9375 to 0.9375
- core: float32 [1024, 1024], replicated, may hold values from -6 to 6
- right_factor: float32 [16384, 1024], P('cols', 'rows'), may hold values from -0.46875 to 0.46875
Outputs:
- core_next: float32 [1024, 1024], replicated
The draws below stay inside these ranges and needn't reach their ends.
All inputs are finite; a program needn't handle non-finite values.
Results may differ from the reference program's by a relative error of at most 0.000062.
Values sent between devices are 32-bit elements; how exact they have to be, the bound alone decides.
A program may use at most 128 MiB of HBM per device.

```python
import math
import jax
import jax.numpy as jnp
from jax import lax

RANK = 1024
PAIRS_ROW = 4096
PAIRS_COL = 16384


def factor_draw(base_key, row_count, salt_value):
    base_key = jax.random.fold_in(base_key, salt_value)
    key_entries, key_scale = jax.random.split(base_key, 2)
    entries = jax.random.truncated_normal(key_entries, -4.0, 4.0, (row_count, RANK), jnp.float32)
    rise_total = 3.5
    row_scale = jnp.exp(jax.random.uniform(key_scale, (row_count, 1), jnp.float32, math.log(0.2), math.log(0.8)))
    position = jnp.arange(row_count, dtype=jnp.float32).reshape(row_count, 1) / float(max(row_count - 1, 1))
    rising = jnp.exp(math.log(rise_total) * position)
    return entries * row_scale * rising / math.sqrt(row_count)


def draw_left_factor(key, part):
    return factor_draw(key, PAIRS_ROW, 101)


def draw_right_factor(key, part):
    return factor_draw(key, PAIRS_COL, 202)


def shard_levels(stream_key, shape, cuts, least, largest):
    gain = 1.0
    for dim, shards_of in cuts:
        steps = jax.random.uniform(jax.random.fold_in(jax.random.fold_in(stream_key, 6), dim), (shards_of,), jnp.float32, least / len(cuts), largest / len(cuts))
        gain = gain * jnp.repeat(jnp.exp(steps), shape[dim] // shards_of).reshape((-1,) + (1,) * (len(shape) - 1 - dim))
    return gain


def bell_draw(own_key, extent, spread, limit, shards=(), held_as=jnp.bfloat16):
    values = jax.random.normal(own_key, extent, jnp.float32) * spread
    if len(shards) > 0:
        values = shard_levels(own_key, extent, shards, -0.22, 0.18) * values
    return jnp.clip(values, min=-limit, max=limit).astype(held_as)


def setup_inputs(seed: int = 0) -> dict:
    key_of = jax.random.split(jax.random.key(seed), 5)
    return {
        "pair_integrals": bell_draw(key_of[0], (PAIRS_ROW, PAIRS_COL), 1.0, 6.0, ((0, 4), (1, 32)), jnp.float32),
        "left_factor": draw_left_factor(jax.random.fold_in(key_of[4], 71), 0),
        "core": bell_draw(key_of[2], (RANK, RANK), 1.0, 6.0, (), jnp.float32),
        "right_factor": draw_right_factor(jax.random.fold_in(key_of[4], 71), 0),
    }


def reference(pair_integrals, left_factor, core, right_factor):
    highest = lax.Precision.HIGHEST
    mixed = jnp.dot(core, right_factor.T, precision=highest, preferred_element_type=jnp.float32)
    residual = pair_integrals - jnp.dot(left_factor, mixed, precision=highest, preferred_element_type=jnp.float32)
    along = jnp.dot(residual, right_factor, precision=highest, preferred_element_type=jnp.float32)
    gradient = jnp.dot(left_factor.T, along, precision=highest, preferred_element_type=jnp.float32)
    numer = jnp.sum(gradient * gradient)
    inner = jnp.dot(gradient, right_factor.T, precision=highest, preferred_element_type=jnp.float32)
    image = jnp.dot(left_factor, inner, precision=highest, preferred_element_type=jnp.float32)
    denom = jnp.sum(image * image)
    return core + (numer / denom) * gradient
```

```python
import functools

import jax
import jax.numpy as jnp
from jax import lax
from jax.experimental import pallas as pl
from jax.experimental.pallas import tpu as pltpu
from jax.sharding import PartitionSpec as P

MESH = pl.DeviceIdType.MESH
F32, BF16 = jnp.float32, jnp.bfloat16
GROUPS = ((0, 384, "xyz"), (384, 384, "yzx"), (768, 256, "zxy"))
MESSAGES = 160
NN = (((1,), (0,)), ((), ()))
NT = (((1,), (1,)), ((), ()))


def split(v):
    hi = v.astype(BF16)
    return hi, (v - hi.astype(F32)).astype(BF16)


def dot3(ah, al, bh, bl, dims):
    dot = functools.partial(lax.dot_general, dimension_numbers=dims, preferred_element_type=F32)
    return dot(ah, bh) + dot(ah, bl) + dot(al, bh)


def aligned(i, m):
    return pl.multiple_of(i, m)


class Sender:
    def __init__(self, send_sems, recv_sems):
        self.send_sems, self.recv_sems, self.sent = send_sems, recv_sems, []

    def __call__(self, src, dst, peer):
        i = len(self.sent)
        copy = pltpu.make_async_remote_copy(
            src_ref=src,
            dst_ref=dst,
            send_sem=self.send_sems.at[i],
            recv_sem=self.recv_sems.at[i],
            device_id=peer,
            device_id_type=MESH,
        )
        copy.start()
        self.sent.append(copy)
        return copy


def lockstep(generators):
    live = list(generators)
    while live:
        still = []
        for g in live:
            try:
                next(g)
                still.append(g)
            except StopIteration:
                pass
        live = still


def kernel(
    v_hbm, l_hbm, z_hbm, r_hbm, g_hbm, step_ref,
    l_in, v_in, z_in, lt, r4, rest, u, u_in, g,
    zh, zl, rh, rl, lth, ltl, mh, ml, resh, resl, uh, ul, gch, gcl, ih, il,
    gp_a, gp_b, gp_c, relay_a, relay_b, relay_c, ra_a, ra_b, ra_c,
    acc_a, acc_b, acc_c, rb_a, rb_b, rb_c, accb_a, accb_b, accb_c, rc_a, rc_b, rc_c,
    slots, send_sems, recv_sems, local_sems,
):
    r, c = lax.axis_index("rows"), lax.axis_index("cols")
    core, z_lo, z_hi = lax.rem(r, 2), lax.div(r, 2), lax.rem(c, 2)
    x, y, z = lax.rem(lax.div(c, 2), 4), lax.div(c, 8), 2 * z_hi + z_lo
    other = 1 - core

    def device(dx, dy, dz, k):
        xx, yy, zz = lax.rem(x + dx, 4), lax.rem(y + dy, 4), lax.rem(z + dz, 4)
        return (2 * lax.rem(zz, 2) + k, 8 * yy + 2 * xx + lax.div(zz, 2))

    peer = {
        "x": [device(d, 0, 0, core) for d in range(4)],
        "y": [device(0, d, 0, core) for d in range(4)],
        "z": [device(0, 0, d, core) for d in range(4)],
    }
    coord = {"x": x, "y": y, "z": z}
    partner = device(0, 0, 0, other)
    z_lo_partner = (2 * (1 - z_lo) + core, c)
    z_hi_partner = peer["z"][2]
    first = [device(d * other, d * core, 0, core) for d in range(4)]
    second = [device(d * core, d * other, 0, core) for d in range(4)]
    i1, i2 = x * other + y * core, y * other + x * core

    copy_l = pltpu.make_async_copy(l_hbm, l_in, local_sems.at[0])
    copy_r = pltpu.make_async_copy(r_hbm, r4.at[r], local_sems.at[1])
    copy_v = pltpu.make_async_copy(v_hbm, v_in, local_sems.at[2])
    copy_l.start()
    copy_r.start()
    copy_v.start()
    copy_z = []
    for b in range(16):
        by, bx = b // 4, b % 4
        at2, at1 = by * other + bx * core, bx * other + by * core
        copy_z.append(
            pltpu.make_async_copy(
                z_hbm.at[pl.ds(64 * b, 64), :],
                z_in.at[at2, pl.ds(aligned(64 * at1, 64), 64), :],
                local_sems.at[4 + b],
            )
        )
        copy_z[-1].start()

    barrier = pltpu.get_barrier_semaphore()
    greeted = [partner] + [peer[a][d] for a in "xyz" for d in (1, 2, 3)]
    for other_device in greeted:
        pl.semaphore_signal(barrier, inc=1, device_id=other_device, device_id_type=MESH)
    pl.semaphore_wait(barrier, len(greeted))

    send = Sender(send_sems, recv_sems)

    def shard(d1, d2, h):
        at1, at2 = lax.rem(i1 + d1, 4), lax.rem(i2 + d2, 4)
        return lt.at[at2, pl.ds(aligned(64 * at1 + 32 * h, 32), 32), :]

    def spread(ref, peers):
        return send(ref, ref, peers[1]), send(ref, ref, peers[3])

    own, far = z_hi, 1 - z_hi
    copy_l.wait()
    lt[i2, pl.ds(aligned(64 * i1 + 32 * own, 32), 32), :] = jnp.transpose(l_in[...])
    mine = shard(0, 0, own)
    to_z = send(mine, mine, z_hi_partner)
    near_own = spread(mine, first)
    wide = {(0, "own"): spread(mine, second)}

    copy_r.wait()
    r_to_core = send(r4.at[r], r4.at[r], partner)
    r_to_z = send(r4.at[r], r4.at[r], z_lo_partner)

    def transpose_v(i):
        rest[:, 128 * i : 128 * i + 128] = jnp.transpose(v_in[128 * i : 128 * i + 128, :])

    copy_v.wait()
    for i in range(4):
        transpose_v(i)

    to_z.wait_recv()
    theirs = shard(0, 0, far)
    near_far = spread(theirs, first)
    wide[0, "far"] = spread(theirs, second)
    for i in range(4, 8):
        transpose_v(i)

    near_own[0].wait_recv()
    ref = shard(3, 0, own)
    through_own = send(ref, ref, first[1])
    wide[3, "own"] = spread(ref, second)
    near_own[1].wait_recv()
    wide[1, "own"] = spread(shard(1, 0, own), second)
    near_far[1].wait_recv()
    ref = shard(1, 0, far)
    through_far = send(ref, ref, first[3])
    wide[1, "far"] = spread(ref, second)
    near_far[0].wait_recv()
    wide[3, "far"] = spread(shard(3, 0, far), second)

    passed = []

    def pass_on(d1):
        wide[d1, "own"][0].wait_recv()
        ref = shard(d1, 3, own)
        passed.append(send(ref, ref, second[1]))
        wide[d1, "far"][1].wait_recv()
        ref = shard(d1, 1, far)
        passed.append(send(ref, ref, second[3]))

    for copy in copy_z:
        copy.wait()

    def split_z(i, _):
        zh[i], zl[i] = split(z_in[i])
        return 0

    lax.fori_loop(0, 4, split_z, 0)

    pass_on(0)
    through_own.wait_recv()
    wide[2, "own"] = spread(shard(2, 0, own), second)
    through_far.wait_recv()
    wide[2, "far"] = spread(shard(2, 0, far), second)

    r_to_z.wait_recv()
    r_far = r4.at[2 * (1 - z_lo) + core]
    r_on = send(r_far, r_far, partner)
    pass_on(3)
    r_to_core.wait_recv()
    r_on.wait_recv()

    def split_r(i, _):
        rh[i], rl[i] = split(r4[i])
        return 0

    lax.fori_loop(0, 4, split_r, 0)

    def times_right(bh, bl):
        total = None
        for s in range(4):
            cols = slice(256 * s, 256 * s + 256)
            term = dot3(rh[s], rl[s], bh[:, cols], bl[:, cols], NT)
            total = term if total is None else total + term
        return total

    def mix(i, _):
        mh[i], ml[i] = split(times_right(zh.at[i], zl.at[i]))
        return 0

    mix(i2, 0)
    pass_on(1)
    mix(lax.rem(i2 + 3, 4), 0)
    mix(lax.rem(i2 + 1, 4), 0)

    def subtract(i):
        lth[i], ltl[i] = split(lt[i])
        for n in range(0, 1024, 256):
            cols = slice(n, n + 256)
            rest[:, cols] -= dot3(mh[i], ml[i], lth[i, :, cols], ltl[i, :, cols], NN)

    subtract(i2)
    pass_on(2)
    mix(lax.rem(i2 + 2, 4), 0)
    for d1 in range(4):
        wide[d1, "far"][0].wait_recv()
    subtract(lax.rem(i2 + 3, 4))
    for d1 in range(4):
        wide[d1, "own"][1].wait_recv()
    subtract(lax.rem(i2 + 1, 4))
    for copy in passed:
        copy.wait_recv()
    subtract(lax.rem(i2 + 2, 4))

    def split_rest(i, _):
        rows = pl.ds(aligned(128 * i, 128), 128)
        resh[rows, :], resl[rows, :] = split(rest[rows, :])
        return 0

    lax.fori_loop(0, 4, split_rest, 0)

    def project(yy):
        for i in range(2):
            parts = []
            for j in (2 * i, 2 * i + 1):
                at2, at1 = yy * other + j * core, j * other + yy * core
                rows = pl.ds(aligned(64 * at1, 64), 64)
                parts.append((lth[at2, rows, :], ltl[at2, rows, :]))
            ah = jnp.concatenate([p[0] for p in parts], axis=0)
            al = jnp.concatenate([p[1] for p in parts], axis=0)
            u[yy, 128 * i : 128 * i + 128, :] = dot3(ah, al, resh[...], resl[...], NT)

    u_sent = []
    for j in range(2):
        project(2 * other + j)
        u_sent.append(send(u.at[2 * other + j], u_in.at[j], partner))
    for j in range(2):
        project(2 * core + j)
    for j in range(2):
        u_sent[j].wait_recv()
        uh[256 * j : 256 * j + 256, :], ul[256 * j : 256 * j + 256, :] = split(u[2 * core + j] + u_in[j])

    def term(s):
        return dot3(uh[...], ul[...], rh[s], rl[s], NN)

    gp_a[:, :256] = term(0)
    second_part = term(1)
    gp_a[:, 256:] = second_part[:, :128]
    gp_b[:, :128] = second_part[:, 128:]
    gp_b[:, 128:] = term(2)
    gp_c[...] = term(3)

    def gradient(n0, w, order, gp, relay, ra, acc, rb, accb, rc):
        a, b, e = order
        ia, ib, ie = coord[a], coord[b], coord[e]
        cols = pl.ds(n0, w)
        opposite, after, before = (aligned(128 * lax.rem(ia + d, 4), 128) for d in (2, 1, 3))
        m1 = send(gp.at[pl.ds(opposite, 64), :], relay.at[0], peer[a][1])
        m2 = send(gp.at[pl.ds(aligned(opposite + 64, 64), 64), :], relay.at[1], peer[a][3])
        m3 = send(gp.at[pl.ds(aligned(after + 64, 64), 64), :], ra.at[0, pl.ds(64, 64), :], peer[a][1])
        m4 = send(gp.at[pl.ds(before, 64), :], ra.at[1, pl.ds(0, 64), :], peer[a][3])
        yield
        m1.wait_recv()
        rows = pl.ds(after, 64)
        gp[rows, :] += relay[0]
        m5 = send(gp.at[rows, :], ra.at[0, pl.ds(0, 64), :], peer[a][1])
        m2.wait_recv()
        rows = pl.ds(aligned(before + 64, 64), 64)
        gp[rows, :] += relay[1]
        m6 = send(gp.at[rows, :], ra.at[1, pl.ds(64, 64), :], peer[a][3])
        yield
        for m in (m3, m4, m5, m6):
            m.wait_recv()
        acc[...] = gp[pl.ds(aligned(128 * ia, 128), 128), :] + ra[0] + ra[1]
        ms = []
        for d in (1, 2, 3):
            rows = pl.ds(aligned(32 * lax.rem(ib + d, 4), 32), 32)
            ms.append(send(acc.at[rows, :], rb.at[d - 1], peer[b][d]))
        yield
        for m in ms:
            m.wait_recv()
        accb[...] = acc[pl.ds(aligned(32 * ib, 32), 32), :] + rb[0] + rb[1] + rb[2]
        ms = []
        for d in (1, 2, 3):
            rows = pl.ds(aligned(8 * lax.rem(ie + d, 4), 8), 8)
            ms.append(send(accb.at[rows, :], rc.at[d - 1], peer[e][d]))
        yield
        for m in ms:
            m.wait_recv()
        base = 512 * core + 128 * ia
        at = pl.ds(aligned(base + 32 * ib + 8 * ie, 8), 8)
        g[at, n0 : n0 + w] = accb[pl.ds(aligned(8 * ie, 8), 8), :] + rc[0] + rc[1] + rc[2]
        ms = [send(g.at[at, cols], g.at[at, cols], peer[e][d]) for d in (1, 2, 3)]
        yield
        for m in ms:
            m.wait_recv()
        at = pl.ds(aligned(base + 32 * ib, 32), 32)
        ms = [send(g.at[at, cols], g.at[at, cols], peer[b][d]) for d in (1, 2, 3)]
        yield
        for m in ms:
            m.wait_recv()
        at = g.at[pl.ds(aligned(base, 128), 128), cols]
        right, left = send(at, at, peer[a][1]), send(at, at, peer[a][3])
        over = [send(at, at, partner)]
        yield
        right.wait_recv()
        row = 512 * core + before
        at = g.at[pl.ds(aligned(row, 64), 64), cols]
        on_right = send(at, at, peer[a][1])
        at = g.at[pl.ds(aligned(row, 128), 128), cols]
        over.append(send(at, at, partner))
        left.wait_recv()
        row = 512 * core + after
        at = g.at[pl.ds(aligned(row + 64, 64), 64), cols]
        on_left = send(at, at, peer[a][3])
        at = g.at[pl.ds(aligned(row, 128), 128), cols]
        over.append(send(at, at, partner))
        yield
        on_right.wait_recv()
        on_left.wait_recv()
        at = g.at[pl.ds(aligned(512 * core + opposite, 128), 128), cols]
        over.append(send(at, at, partner))
        yield
        for m in over:
            m.wait_recv()

    buffers = (
        (gp_a, relay_a, ra_a, acc_a, rb_a, accb_a, rc_a),
        (gp_b, relay_b, ra_b, acc_b, rb_b, accb_b, rc_b),
        (gp_c, relay_c, ra_c, acc_c, rb_c, accb_c, rc_c),
    )
    lockstep(gradient(*group, *held) for group, held in zip(GROUPS, buffers))

    copy_g = pltpu.make_async_copy(g, g_hbm, local_sems.at[3])
    copy_g.start()

    rest[...] = jnp.zeros_like(rest)

    def image(i, _):
        for j in range(4):
            row = 64 * (i * (4 - 3 * core) + j * (1 + 3 * core))
            rows = slice(64 * j, 64 * j + 64)
            gch[rows, :], gcl[rows, :] = split(g[pl.ds(aligned(row, 64), 64), :])
        ih[...], il[...] = split(times_right(gch, gcl))
        for n in range(0, 1024, 256):
            cols = slice(n, n + 256)
            rest[:, cols] += dot3(ih[...], il[...], lth[i, :, cols], ltl[i, :, cols], NN)
        return 0

    lax.fori_loop(0, 4, image, 0)

    def squares(ref, rows_in_all):
        def body(i, total):
            part = ref[pl.ds(aligned(32 * i, 32), 32), :]
            part = part * part
            return total + jnp.sum(part.reshape(4, 8, 1024), axis=0)

        total = lax.fori_loop(0, rows_in_all // 32, body, jnp.zeros((8, 1024), F32))
        return functools.reduce(jnp.add, [total[:, 128 * i : 128 * i + 128] for i in range(8)])

    slots[3, core] = squares(rest, 512)
    ms = [send(slots.at[3, core], slots.at[3, core], partner)]
    numer = squares(g, 1024)
    for n, a in enumerate("xyz"):
        for m in ms:
            m.wait_recv()
        before = slots[3, 0] + slots[3, 1] if n == 0 else functools.reduce(jnp.add, [slots[n - 1, i] for i in range(4)])
        slots[n, coord[a]] = before
        at = slots.at[n, coord[a]]
        ms = [send(at, at, peer[a][d]) for d in (1, 2, 3)]
    for m in ms:
        m.wait_recv()
    denom = functools.reduce(jnp.add, [slots[2, i] for i in range(4)])
    total = lambda v: jnp.sum(jnp.sum(v, axis=0, keepdims=True), axis=1, keepdims=True)
    step_ref[...] = jnp.broadcast_to(total(numer) / total(denom), (8, 128))

    copy_g.wait()
    for copy in send.sent:
        copy.wait_send()


def scratch():
    v = pltpu.VMEM
    groups = [w for _, w, _ in GROUPS]
    return [
        v((1024, 32), F32), v((1024, 512), F32), v((4, 256, 1024), F32), v((4, 256, 1024), F32),
        v((4, 512, 256), F32), v((512, 1024), F32), v((4, 256, 512), F32), v((2, 256, 512), F32), v((1024, 1024), F32),
        v((4, 256, 1024), BF16), v((4, 256, 1024), BF16), v((4, 512, 256), BF16), v((4, 512, 256), BF16),
        v((4, 256, 1024), BF16), v((4, 256, 1024), BF16), v((4, 512, 256), BF16), v((4, 512, 256), BF16),
        v((512, 1024), BF16), v((512, 1024), BF16), v((512, 512), BF16), v((512, 512), BF16),
        v((256, 1024), BF16), v((256, 1024), BF16), v((512, 256), BF16), v((512, 256), BF16),
        *[v((512, w), F32) for w in groups], *[v((2, 64, w), F32) for w in groups],
        *[v((2, 128, w), F32) for w in groups], *[v((128, w), F32) for w in groups],
        *[v((3, 32, w), F32) for w in groups], *[v((32, w), F32) for w in groups],
        *[v((3, 8, w), F32) for w in groups],
        v((4, 4, 8, 128), F32),
        pltpu.SemaphoreType.DMA((MESSAGES,)), pltpu.SemaphoreType.DMA((MESSAGES,)), pltpu.SemaphoreType.DMA((20,)),
    ]


def shards(pair_integrals, left_factor, core, right_factor):
    gradient, step = pl.pallas_call(
        kernel,
        out_shape=(jax.ShapeDtypeStruct((1024, 1024), F32), jax.ShapeDtypeStruct((8, 128), F32)),
        in_specs=[pl.BlockSpec(memory_space=pl.ANY)] * 4,
        out_specs=(pl.BlockSpec(memory_space=pl.ANY), pl.BlockSpec(memory_space=pltpu.VMEM)),
        scratch_shapes=scratch(),
        compiler_params=pltpu.CompilerParams(
            collective_id=0, has_side_effects=True, vmem_limit_bytes=60 * 1024 * 1024
        ),
        cost_estimate=pl.CostEstimate(flops=7 * 10**9, bytes_accessed=16 * 2**20, transcendentals=0),
    )(pair_integrals, left_factor, core, right_factor)
    return core + step[0, 0] * gradient


def solution(mesh):
    placed = (P("rows", "cols"), P("rows", "cols"), P(), P("cols", "rows"))
    return jax.shard_map(shards, mesh=mesh, in_specs=placed, out_specs=P(), check_vma=False)
```

```python
import functools

import jax
import jax.numpy as jnp
from jax import lax
from jax.experimental import pallas as pl
from jax.experimental.pallas import tpu as pltpu
from jax.sharding import PartitionSpec as P

MESH = pl.DeviceIdType.MESH
F32, BF16 = jnp.float32, jnp.bfloat16
GROUPS = ((0, 384, "xyz"), (384, 384, "yzx"), (768, 256, "zxy"))
MESSAGES = 160
NN = (((1,), (0,)), ((), ()))
NT = (((1,), (1,)), ((), ()))


def split(v):
    hi = v.astype(BF16)
    return hi, (v - hi.astype(F32)).astype(BF16)


def dot3(ah, al, bh, bl, dims):
    (da,), (db,) = dims[0]
    return lax.dot_general(
        jnp.concatenate([ah, ah, al], da),
        jnp.concatenate([bh, bl, bh], db),
        dimension_numbers=dims,
        preferred_element_type=F32,
    )


def aligned(i, m):
    return pl.multiple_of(i, m)


class Sender:
    def __init__(self, send_sems, recv_sems):
        self.send_sems, self.recv_sems, self.sent = send_sems, recv_sems, []

    def __call__(self, src, dst, peer):
        i = len(self.sent)
        copy = pltpu.make_async_remote_copy(
            src_ref=src,
            dst_ref=dst,
            send_sem=self.send_sems.at[i],
            recv_sem=self.recv_sems.at[i],
            device_id=peer,
            device_id_type=MESH,
        )
        copy.start()
        self.sent.append(copy)
        return copy


def lockstep(generators):
    live = list(generators)
    while live:
        still = []
        for g in live:
            try:
                next(g)
                still.append(g)
            except StopIteration:
                pass
        live = still


def kernel(
    v_hbm, l_hbm, z_hbm, r_hbm, out,
    v_in, z_in, lt, r4, rest, u, u_in, g,
    zh, zl, rh, rl, lth, ltl, mh, ml, resh, resl, uh, ul, gch, gcl, ih, il,
    gp_a, gp_b, gp_c, relay_a, relay_b, relay_c, ra_a, ra_b, ra_c,
    acc_a, acc_b, acc_c, rb_a, rb_b, rb_c, accb_a, accb_b, accb_c, rc_a, rc_b, rc_c,
    slots, send_sems, recv_sems, local_sems,
):
    r, c = lax.axis_index("rows"), lax.axis_index("cols")
    core, z_lo, z_hi = lax.rem(r, 2), lax.div(r, 2), lax.rem(c, 2)
    x, y, z = lax.rem(lax.div(c, 2), 4), lax.div(c, 8), 2 * z_hi + z_lo
    other = 1 - core

    def device(dx, dy, dz, k):
        xx, yy, zz = lax.rem(x + dx, 4), lax.rem(y + dy, 4), lax.rem(z + dz, 4)
        return (2 * lax.rem(zz, 2) + k, 8 * yy + 2 * xx + lax.div(zz, 2))

    peer = {
        "x": [device(d, 0, 0, core) for d in range(4)],
        "y": [device(0, d, 0, core) for d in range(4)],
        "z": [device(0, 0, d, core) for d in range(4)],
    }
    coord = {"x": x, "y": y, "z": z}
    partner = device(0, 0, 0, other)
    z_lo_partner = (2 * (1 - z_lo) + core, c)
    z_hi_partner = peer["z"][2]
    first = [device(d * other, d * core, 0, core) for d in range(4)]
    second = [device(d * core, d * other, 0, core) for d in range(4)]
    i1, i2 = x * other + y * core, y * other + x * core

    at_l = (i2, pl.ds(aligned(64 * i1 + 32 * z_hi, 32), 32))
    copy_l = pltpu.make_async_copy(l_hbm, lt.at[at_l], local_sems.at[0])
    copy_r = pltpu.make_async_copy(r_hbm, r4.at[r], local_sems.at[1])
    copy_v = pltpu.make_async_copy(v_hbm, v_in, local_sems.at[2])
    copy_l.start()
    copy_r.start()
    copy_v.start()
    copy_z = []
    for b in range(16):
        by, bx = b // 4, b % 4
        at2, at1 = by * other + bx * core, bx * other + by * core
        copy_z.append(
            pltpu.make_async_copy(
                z_hbm.at[pl.ds(64 * b, 64), :],
                z_in.at[at2, pl.ds(aligned(64 * at1, 64), 64), :],
                local_sems.at[4 + b],
            )
        )
        copy_z[-1].start()

    barrier = pltpu.get_barrier_semaphore()
    greeted = [partner] + [peer[a][d] for a in "xyz" for d in (1, 2, 3)]
    for other_device in greeted:
        pl.semaphore_signal(barrier, inc=1, device_id=other_device, device_id_type=MESH)
    pl.semaphore_wait(barrier, len(greeted))

    send = Sender(send_sems, recv_sems)

    def shard(d1, d2, h):
        at1, at2 = lax.rem(i1 + d1, 4), lax.rem(i2 + d2, 4)
        return lt.at[at2, pl.ds(aligned(64 * at1 + 32 * h, 32), 32), :]

    def spread(ref, peers):
        return send(ref, ref, peers[1]), send(ref, ref, peers[3])

    own, far = z_hi, 1 - z_hi
    copy_l.wait()
    mine = shard(0, 0, own)
    to_z = send(mine, mine, z_hi_partner)
    near_own = spread(mine, first)
    wide = {(0, "own"): spread(mine, second)}

    copy_r.wait()
    r_to_core = send(r4.at[r], r4.at[r], partner)
    r_to_z = send(r4.at[r], r4.at[r], z_lo_partner)

    def transpose_v(i):
        rest[:, 128 * i : 128 * i + 128] = jnp.transpose(v_in[128 * i : 128 * i + 128, :])

    copy_v.wait()
    for i in range(4):
        transpose_v(i)

    to_z.wait_recv()
    theirs = shard(0, 0, far)
    near_far = spread(theirs, first)
    wide[0, "far"] = spread(theirs, second)
    for i in range(4, 8):
        transpose_v(i)

    near_own[0].wait_recv()
    ref = shard(3, 0, own)
    through_own = send(ref, ref, first[1])
    wide[3, "own"] = spread(ref, second)
    near_own[1].wait_recv()
    wide[1, "own"] = spread(shard(1, 0, own), second)
    near_far[1].wait_recv()
    ref = shard(1, 0, far)
    through_far = send(ref, ref, first[3])
    wide[1, "far"] = spread(ref, second)
    near_far[0].wait_recv()
    wide[3, "far"] = spread(shard(3, 0, far), second)

    passed = []

    def pass_on(d1):
        wide[d1, "own"][0].wait_recv()
        ref = shard(d1, 3, own)
        passed.append(send(ref, ref, second[1]))
        wide[d1, "far"][1].wait_recv()
        ref = shard(d1, 1, far)
        passed.append(send(ref, ref, second[3]))

    for copy in copy_z:
        copy.wait()

    def split_z(i, _):
        zh[i], zl[i] = split(z_in[i])
        return 0

    lax.fori_loop(0, 4, split_z, 0)

    pass_on(0)
    through_own.wait_recv()
    wide[2, "own"] = spread(shard(2, 0, own), second)
    through_far.wait_recv()
    wide[2, "far"] = spread(shard(2, 0, far), second)

    r_to_z.wait_recv()
    r_far = r4.at[2 * (1 - z_lo) + core]
    r_on = send(r_far, r_far, partner)
    pass_on(3)
    r_to_core.wait_recv()
    r_on.wait_recv()

    for i in range(4):
        cols = slice(256 * i, 256 * i + 256)
        rh[:, cols], rl[:, cols] = split(r4[i])

    def times_right(m, bh, bl):
        rows = slice(m, m + 256)
        return split(dot3(rh[rows, :], rl[rows, :], bh[...], bl[...], NT))

    def mix(i, _):
        for m in (0, 256):
            mh[i, m : m + 256, :], ml[i, m : m + 256, :] = times_right(m, zh.at[i], zl.at[i])
        return 0

    mix(i2, 0)
    pass_on(1)
    mix(lax.rem(i2 + 3, 4), 0)
    mix(lax.rem(i2 + 1, 4), 0)

    def subtract(i):
        lth[i], ltl[i] = split(lt[i])
        for n in range(0, 1024, 256):
            cols = slice(n, n + 256)
            rest[:, cols] -= dot3(mh[i], ml[i], lth[i, :, cols], ltl[i, :, cols], NN)

    subtract(i2)
    pass_on(2)
    mix(lax.rem(i2 + 2, 4), 0)
    for d1 in range(4):
        wide[d1, "far"][0].wait_recv()
    subtract(lax.rem(i2 + 3, 4))
    for d1 in range(4):
        wide[d1, "own"][1].wait_recv()
    subtract(lax.rem(i2 + 1, 4))
    for copy in passed:
        copy.wait_recv()
    subtract(lax.rem(i2 + 2, 4))

    def split_rest(i, _):
        rows = pl.ds(aligned(128 * i, 128), 128)
        resh[rows, :], resl[rows, :] = split(rest[rows, :])
        return 0

    lax.fori_loop(0, 4, split_rest, 0)

    def project(yy):
        parts = []
        for j in range(4):
            at2, at1 = yy * other + j * core, j * other + yy * core
            rows = pl.ds(aligned(64 * at1, 64), 64)
            parts.append((lth[at2, rows, :], ltl[at2, rows, :]))
        ah = jnp.concatenate([p[0] for p in parts], axis=0)
        al = jnp.concatenate([p[1] for p in parts], axis=0)
        u[yy] = dot3(ah, al, resh[...], resl[...], NT)

    u_sent = []
    for j in range(2):
        project(2 * other + j)
        u_sent.append(send(u.at[2 * other + j], u_in.at[j], partner))
    for j in range(2):
        project(2 * core + j)
    for j in range(2):
        u_sent[j].wait_recv()
        uh[256 * j : 256 * j + 256, :], ul[256 * j : 256 * j + 256, :] = split(u[2 * core + j] + u_in[j])

    for m in (0, 256):
        rows = slice(m, m + 256)
        for s in range(4):
            cols = slice(256 * s, 256 * s + 256)
            term = dot3(uh[rows, :], ul[rows, :], rh[:, cols], rl[:, cols], NN)
            if s == 0:
                gp_a[rows, :256] = term
            elif s == 1:
                gp_a[rows, 256:] = term[:, :128]
                gp_b[rows, :128] = term[:, 128:]
            elif s == 2:
                gp_b[rows, 128:] = term
            else:
                gp_c[rows, :] = term

    def gradient(n0, w, order, gp, relay, ra, acc, rb, accb, rc):
        a, b, e = order
        ia, ib, ie = coord[a], coord[b], coord[e]
        cols = pl.ds(n0, w)
        opposite, after, before = (aligned(128 * lax.rem(ia + d, 4), 128) for d in (2, 1, 3))
        m1 = send(gp.at[pl.ds(opposite, 64), :], relay.at[0], peer[a][1])
        m2 = send(gp.at[pl.ds(aligned(opposite + 64, 64), 64), :], relay.at[1], peer[a][3])
        m3 = send(gp.at[pl.ds(aligned(after + 64, 64), 64), :], ra.at[0, pl.ds(64, 64), :], peer[a][1])
        m4 = send(gp.at[pl.ds(before, 64), :], ra.at[1, pl.ds(0, 64), :], peer[a][3])
        yield
        m1.wait_recv()
        rows = pl.ds(after, 64)
        gp[rows, :] += relay[0]
        m5 = send(gp.at[rows, :], ra.at[0, pl.ds(0, 64), :], peer[a][1])
        m2.wait_recv()
        rows = pl.ds(aligned(before + 64, 64), 64)
        gp[rows, :] += relay[1]
        m6 = send(gp.at[rows, :], ra.at[1, pl.ds(64, 64), :], peer[a][3])
        yield
        for m in (m3, m4, m5, m6):
            m.wait_recv()
        acc[...] = gp[pl.ds(aligned(128 * ia, 128), 128), :] + ra[0] + ra[1]
        ms = []
        for d in (1, 2, 3):
            rows = pl.ds(aligned(32 * lax.rem(ib + d, 4), 32), 32)
            ms.append(send(acc.at[rows, :], rb.at[d - 1], peer[b][d]))
        yield
        for m in ms:
            m.wait_recv()
        accb[...] = acc[pl.ds(aligned(32 * ib, 32), 32), :] + rb[0] + rb[1] + rb[2]
        ms = []
        for d in (1, 2, 3):
            rows = pl.ds(aligned(8 * lax.rem(ie + d, 4), 8), 8)
            ms.append(send(accb.at[rows, :], rc.at[d - 1], peer[e][d]))
        yield
        for m in ms:
            m.wait_recv()
        base = 512 * core + 128 * ia
        at = pl.ds(aligned(base + 32 * ib + 8 * ie, 8), 8)
        g[at, n0 : n0 + w] = accb[pl.ds(aligned(8 * ie, 8), 8), :] + rc[0] + rc[1] + rc[2]
        ms = [send(g.at[at, cols], g.at[at, cols], peer[e][d]) for d in (1, 2, 3)]
        yield
        for m in ms:
            m.wait_recv()
        at = pl.ds(aligned(base + 32 * ib, 32), 32)
        ms = [send(g.at[at, cols], g.at[at, cols], peer[b][d]) for d in (1, 2, 3)]
        yield
        for m in ms:
            m.wait_recv()
        at = g.at[pl.ds(aligned(base, 128), 128), cols]
        right, left = send(at, at, peer[a][1]), send(at, at, peer[a][3])
        over = [send(at, at, partner)]
        yield
        right.wait_recv()
        row = 512 * core + before
        at = g.at[pl.ds(aligned(row, 64), 64), cols]
        on_right = send(at, at, peer[a][1])
        at = g.at[pl.ds(aligned(row, 128), 128), cols]
        over.append(send(at, at, partner))
        left.wait_recv()
        row = 512 * core + after
        at = g.at[pl.ds(aligned(row + 64, 64), 64), cols]
        on_left = send(at, at, peer[a][3])
        at = g.at[pl.ds(aligned(row, 128), 128), cols]
        over.append(send(at, at, partner))
        yield
        on_right.wait_recv()
        on_left.wait_recv()
        at = g.at[pl.ds(aligned(512 * core + opposite, 128), 128), cols]
        over.append(send(at, at, partner))
        yield
        for m in over:
            m.wait_recv()

    buffers = (
        (gp_a, relay_a, ra_a, acc_a, rb_a, accb_a, rc_a),
        (gp_b, relay_b, ra_b, acc_b, rb_b, accb_b, rc_b),
        (gp_c, relay_c, ra_c, acc_c, rb_c, accb_c, rc_c),
    )
    lockstep(gradient(*group, *held) for group, held in zip(GROUPS, buffers))

    rest[...] = jnp.zeros_like(rest)

    def image(i, _):
        for j in range(4):
            row = 64 * (i * (4 - 3 * core) + j * (1 + 3 * core))
            rows = slice(64 * j, 64 * j + 64)
            gch[rows, :], gcl[rows, :] = split(g[pl.ds(aligned(row, 64), 64), :])
        for m in (0, 256):
            ih[m : m + 256, :], il[m : m + 256, :] = times_right(m, gch, gcl)
        for n in range(0, 1024, 256):
            cols = slice(n, n + 256)
            rest[:, cols] += dot3(ih[...], il[...], lth[i, :, cols], ltl[i, :, cols], NN)
        return 0

    lax.fori_loop(0, 4, image, 0)

    def squares(ref, rows_in_all):
        def body(i, total):
            part = ref[pl.ds(aligned(32 * i, 32), 32), :]
            part = part * part
            return total + jnp.sum(part.reshape(4, 8, 1024), axis=0)

        total = lax.fori_loop(0, rows_in_all // 32, body, jnp.zeros((8, 1024), F32))
        return functools.reduce(jnp.add, [total[:, 128 * i : 128 * i + 128] for i in range(8)])

    slots[3, core] = squares(rest, 512)
    ms = [send(slots.at[3, core], slots.at[3, core], partner)]
    numer = squares(g, 1024)
    for n, a in enumerate("xyz"):
        for m in ms:
            m.wait_recv()
        before = slots[3, 0] + slots[3, 1] if n == 0 else functools.reduce(jnp.add, [slots[n - 1, i] for i in range(4)])
        slots[n, coord[a]] = before
        at = slots.at[n, coord[a]]
        ms = [send(at, at, peer[a][d]) for d in (1, 2, 3)]
    for m in ms:
        m.wait_recv()
    denom = functools.reduce(jnp.add, [slots[2, i] for i in range(4)])
    total = lambda v: jnp.sum(jnp.sum(v, axis=0, keepdims=True), axis=1, keepdims=True)
    step = total(numer) / total(denom)

    def update(b, _):
        by, bx = lax.div(b, 4), lax.rem(b, 4)
        at2, at1 = by * other + bx * core, bx * other + by * core
        rows = pl.ds(aligned(64 * b, 64), 64)
        out[rows, :] = z_in[at2, pl.ds(aligned(64 * at1, 64), 64), :] + step * g[rows, :]
        return 0

    lax.fori_loop(0, 16, update, 0)

    for copy in send.sent:
        copy.wait_send()


def scratch():
    v = pltpu.VMEM
    groups = [w for _, w, _ in GROUPS]
    return [
        v((1024, 512), F32), v((4, 256, 1024), F32), v((4, 256, 1024), F32),
        v((4, 512, 256), F32), v((512, 1024), F32), v((4, 256, 512), F32), v((2, 256, 512), F32), v((1024, 1024), F32),
        v((4, 256, 1024), BF16), v((4, 256, 1024), BF16), v((512, 1024), BF16), v((512, 1024), BF16),
        v((4, 256, 1024), BF16), v((4, 256, 1024), BF16), v((4, 512, 256), BF16), v((4, 512, 256), BF16),
        v((512, 1024), BF16), v((512, 1024), BF16), v((512, 512), BF16), v((512, 512), BF16),
        v((256, 1024), BF16), v((256, 1024), BF16), v((512, 256), BF16), v((512, 256), BF16),
        *[v((512, w), F32) for w in groups], *[v((2, 64, w), F32) for w in groups],
        *[v((2, 128, w), F32) for w in groups], *[v((128, w), F32) for w in groups],
        *[v((3, 32, w), F32) for w in groups], *[v((32, w), F32) for w in groups],
        *[v((3, 8, w), F32) for w in groups],
        v((4, 4, 8, 128), F32),
        pltpu.SemaphoreType.DMA((MESSAGES,)), pltpu.SemaphoreType.DMA((MESSAGES,)), pltpu.SemaphoreType.DMA((20,)),
    ]


def shards(pair_integrals, left_factor, core, right_factor):
    in_hbm = functools.partial(pltpu.with_memory_space_constraint, memory_space=pltpu.HBM)
    return pl.pallas_call(
        kernel,
        out_shape=pltpu.VMEM((1024, 1024), F32),
        in_specs=[pl.BlockSpec(memory_space=pltpu.HBM)] * 4,
        out_specs=pl.BlockSpec(memory_space=pltpu.VMEM),
        scratch_shapes=scratch(),
        compiler_params=pltpu.CompilerParams(
            collective_id=0, has_side_effects=True, vmem_limit_bytes=54 * 1024 * 1024
        ),
        cost_estimate=pl.CostEstimate(flops=7 * 10**9, bytes_accessed=16 * 2**20, transcendentals=0),
    )(*map(in_hbm, (pair_integrals, left_factor.T, core, right_factor)))


def solution(mesh):
    placed = (P("rows", "cols"), P("rows", "cols"), P(), P("cols", "rows"))
    return jax.shard_map(shards, mesh=mesh, in_specs=placed, out_specs=P(), check_vma=False)
```

```python
import functools

import jax
import jax.numpy as jnp
from jax import lax
from jax.experimental import pallas as pl
from jax.experimental.pallas import tpu as pltpu
from jax.sharding import PartitionSpec as P

MESH = pl.DeviceIdType.MESH
F32, BF16 = jnp.float32, jnp.bfloat16
GROUPS = ((0, 256), (256, 128), (384, 128))
MESSAGES = 160
NN = (((1,), (0,)), ((), ()))
NT = (((1,), (1,)), ((), ()))


def split(v):
    hi = v.astype(BF16)
    return hi, (v - hi.astype(F32)).astype(BF16)


def dot3(ah, al, bh, bl, dims):
    (da,), (db,) = dims[0]
    return lax.dot_general(
        jnp.concatenate([ah, ah, al], da),
        jnp.concatenate([bh, bl, bh], db),
        dimension_numbers=dims,
        preferred_element_type=F32,
    )


def aligned(i, m):
    return pl.multiple_of(i, m)


class Sender:
    def __init__(self, send_sems, recv_sems):
        self.send_sems, self.recv_sems, self.sent = send_sems, recv_sems, []

    def __call__(self, src, dst, peer):
        i = len(self.sent)
        copy = pltpu.make_async_remote_copy(
            src_ref=src,
            dst_ref=dst,
            send_sem=self.send_sems.at[i],
            recv_sem=self.recv_sems.at[i],
            device_id=peer,
            device_id_type=MESH,
        )
        copy.start()
        self.sent.append(copy)
        return copy


def lockstep(generators):
    live = list(generators)
    while live:
        still = []
        for g in live:
            try:
                next(g)
                still.append(g)
            except StopIteration:
                pass
        live = still


def kernel(
    v_hbm, l_hbm, z_hbm, r_hbm, out,
    v_in, z_in, lt, r4, rest, u, u_in, g,
    zh, zl, rh, rl, lth, ltl, mh, ml, resh, resl, uh, ul, inner, ih, il,
    gp, relay, ra, acc, rb, ring, slots_z, slots_xy, send_sems, recv_sems, local_sems,
):
    r, c = lax.axis_index("rows"), lax.axis_index("cols")
    core, z_lo, z_hi = lax.rem(r, 2), lax.div(r, 2), lax.rem(c, 2)
    x, y, z = lax.rem(lax.div(c, 2), 4), lax.div(c, 8), 2 * z_hi + z_lo
    other = 1 - core

    def device(dx, dy, dz, k):
        xx, yy, zz = lax.rem(x + dx, 4), lax.rem(y + dy, 4), lax.rem(z + dz, 4)
        return (2 * lax.rem(zz, 2) + k, 8 * yy + 2 * xx + lax.div(zz, 2))

    partner = device(0, 0, 0, other)
    z_lo_partner = (2 * (1 - z_lo) + core, c)
    z_hi_partner = device(0, 0, 2, core)
    near_z = [device(0, 0, d, k) for d in range(4) for k in (core, other)][1:]
    near_xy = [device(dx, dy, 0, core) for dx in range(4) for dy in range(4)][1:]
    first = [device(d * other, d * core, 0, core) for d in range(4)]
    second = [device(d * core, d * other, 0, core) for d in range(4)]
    i1, i2 = x * other + y * core, y * other + x * core

    at_l = (i2, pl.ds(aligned(64 * i1 + 32 * z_hi, 32), 32))
    copy_l = pltpu.make_async_copy(l_hbm, lt.at[at_l], local_sems.at[0])
    copy_r = pltpu.make_async_copy(r_hbm, r4.at[r], local_sems.at[1])
    copy_v = pltpu.make_async_copy(v_hbm, v_in, local_sems.at[2])
    copy_l.start()
    copy_r.start()
    copy_v.start()
    copy_z = []
    for b in range(16):
        by, bx = b // 4, b % 4
        at2, at1 = by * other + bx * core, bx * other + by * core
        copy_z.append(
            pltpu.make_async_copy(
                z_hbm.at[pl.ds(64 * b, 64), :],
                z_in.at[at2, pl.ds(aligned(64 * at1, 64), 64), :],
                local_sems.at[4 + b],
            )
        )
        copy_z[-1].start()

    barrier = pltpu.get_barrier_semaphore()
    greeted = near_z + near_xy
    for other_device in greeted:
        pl.semaphore_signal(barrier, inc=1, device_id=other_device, device_id_type=MESH)
    pl.semaphore_wait(barrier, len(greeted))

    send = Sender(send_sems, recv_sems)

    def shard(d1, d2, h):
        at1, at2 = lax.rem(i1 + d1, 4), lax.rem(i2 + d2, 4)
        return lt.at[at2, pl.ds(aligned(64 * at1 + 32 * h, 32), 32), :]

    def spread(ref, peers):
        return send(ref, ref, peers[1]), send(ref, ref, peers[3])

    own, far = z_hi, 1 - z_hi
    copy_l.wait()
    mine = shard(0, 0, own)
    to_z = send(mine, mine, z_hi_partner)
    near_own = spread(mine, first)
    wide = {(0, "own"): spread(mine, second)}

    copy_r.wait()
    r_to_core = send(r4.at[r], r4.at[r], partner)
    r_to_z = send(r4.at[r], r4.at[r], z_lo_partner)

    def transpose_v(i):
        rest[:, 128 * i : 128 * i + 128] = jnp.transpose(v_in[128 * i : 128 * i + 128, :])

    copy_v.wait()
    for i in range(4):
        transpose_v(i)

    to_z.wait_recv()
    theirs = shard(0, 0, far)
    near_far = spread(theirs, first)
    wide[0, "far"] = spread(theirs, second)
    for i in range(4, 8):
        transpose_v(i)

    near_own[0].wait_recv()
    ref = shard(3, 0, own)
    through_own = send(ref, ref, first[1])
    wide[3, "own"] = spread(ref, second)
    near_own[1].wait_recv()
    wide[1, "own"] = spread(shard(1, 0, own), second)
    near_far[1].wait_recv()
    ref = shard(1, 0, far)
    through_far = send(ref, ref, first[3])
    wide[1, "far"] = spread(ref, second)
    near_far[0].wait_recv()
    wide[3, "far"] = spread(shard(3, 0, far), second)

    passed = []

    def pass_on(d1):
        wide[d1, "own"][0].wait_recv()
        ref = shard(d1, 3, own)
        passed.append(send(ref, ref, second[1]))
        wide[d1, "far"][1].wait_recv()
        ref = shard(d1, 1, far)
        passed.append(send(ref, ref, second[3]))

    pass_on(0)
    through_own.wait_recv()
    wide[2, "own"] = spread(shard(2, 0, own), second)
    through_far.wait_recv()
    wide[2, "far"] = spread(shard(2, 0, far), second)

    for copy in copy_z:
        copy.wait()

    def split_z(i, _):
        zh[i], zl[i] = split(z_in[i])
        return 0

    lax.fori_loop(0, 4, split_z, 0)
    pass_on(3)
    pass_on(1)

    r_to_z.wait_recv()
    r_far = r4.at[2 * (1 - z_lo) + core]
    r_on = send(r_far, r_far, partner)
    r_to_core.wait_recv()
    r_on.wait_recv()

    def split_r(i, _):
        rh[i], rl[i] = split(r4[i])
        return 0

    lax.fori_loop(0, 4, split_r, 0)

    def mix(i, _):
        for m in (0, 256):
            rows = slice(m, m + 256)
            ah, al = (jnp.concatenate([ref[k, rows, :] for k in range(4)], 1) for ref in (rh, rl))
            mh[i, rows, :], ml[i, rows, :] = split(dot3(ah, al, zh[i], zl[i], NT))
        return 0

    mix(i2, 0)
    mix(lax.rem(i2 + 3, 4), 0)

    def subtract(i):
        lth[i], ltl[i] = split(lt[i])
        for n in range(0, 1024, 256):
            cols = slice(n, n + 256)
            rest[:, cols] -= dot3(mh[i], ml[i], lth[i, :, cols], ltl[i, :, cols], NN)

    pass_on(2)
    mix(lax.rem(i2 + 1, 4), 0)
    mix(lax.rem(i2 + 2, 4), 0)
    subtract(i2)
    for d1 in range(4):
        wide[d1, "far"][0].wait_recv()
    subtract(lax.rem(i2 + 3, 4))
    for d1 in range(4):
        wide[d1, "own"][1].wait_recv()
    subtract(lax.rem(i2 + 1, 4))
    for copy in passed:
        copy.wait_recv()
    subtract(lax.rem(i2 + 2, 4))

    def split_rest(i, _):
        rows = pl.ds(aligned(128 * i, 128), 128)
        resh[rows, :], resl[rows, :] = split(rest[rows, :])
        return 0

    lax.fori_loop(0, 4, split_rest, 0)

    def rank_rows(yy):
        parts = []
        for j in range(4):
            at2, at1 = yy * other + j * core, j * other + yy * core
            rows = pl.ds(aligned(64 * at1, 64), 64)
            parts.append((lth[at2, rows, :], ltl[at2, rows, :]))
        return (jnp.concatenate([p[i] for p in parts], axis=0) for i in (0, 1))

    def project(yy):
        ah, al = rank_rows(yy)
        u[yy] = dot3(ah, al, resh[...], resl[...], NT)

    u_sent = []
    for j in range(2):
        project(2 * other + j)
        u_sent.append(send(u.at[2 * other + j], u_in.at[j], partner))
    for j in range(2):
        project(2 * core + j)
    for j in range(2):
        u_sent[j].wait_recv()
        uh[256 * j : 256 * j + 256, :], ul[256 * j : 256 * j + 256, :] = split(u[2 * core + j] + u_in[j])

    def gradient(n0, w, a, b, e, relay, ra, acc, rb, ring):
        half = w // 2
        ia, ib, ie = (x * v[0] + y * v[1] + z * v[2] for v in (a, b, e))
        towards = lambda v, d: device(d * v[0], d * v[1], d * v[2], core)
        opposite, after, before = (lax.rem(ia + d, 4) for d in (2, 1, 3))
        rows, top, low = pl.ds(n0, w), pl.ds(n0, half), pl.ds(n0 + half, half)

        def term(j):
            gp[j, rows, :] = dot3(uh[rows, :], ul[rows, :], rh[j], rl[j], NN)

        term(opposite)
        m1 = send(gp.at[opposite, top], relay.at[0], towards(a, 1))
        m2 = send(gp.at[opposite, low], relay.at[1], towards(a, 3))
        yield
        term(after)
        m3 = send(gp.at[after, low], ra.at[0, pl.ds(half, half)], towards(a, 1))
        term(before)
        m4 = send(gp.at[before, top], ra.at[1, pl.ds(0, half)], towards(a, 3))
        yield
        m1.wait_recv()
        gp[after, top, :] += relay[0]
        m5 = send(gp.at[after, top], ra.at[0, pl.ds(0, half)], towards(a, 1))
        m2.wait_recv()
        gp[before, low, :] += relay[1]
        m6 = send(gp.at[before, low], ra.at[1, pl.ds(half, half)], towards(a, 3))
        yield
        term(ia)
        yield
        for m in (m3, m4, m5, m6):
            m.wait_recv()
        acc[...] = gp[ia, rows, :] + ra[0] + ra[1]
        quarter = w // 4
        ms = []
        for d in (1, 2, 3):
            part = pl.ds(aligned(quarter * lax.rem(ib + d, 4), quarter), quarter)
            ms.append(send(acc.at[part], rb.at[d - 1], towards(b, d)))
        yield
        for m in ms:
            m.wait_recv()
        ring[ie] = acc[pl.ds(aligned(quarter * ib, quarter), quarter), :] + rb[0] + rb[1] + rb[2]
        ms = [send(ring.at[ie], ring.at[ie], towards(e, d)) for d in (1, 2, 3)]
        yield
        for m in ms:
            m.wait_recv()
        base = 512 * core + n0
        part = pl.ds(aligned(base + quarter * ib, quarter), quarter)
        g[ia, part, :] = ring[0] + ring[1] + ring[2] + ring[3]
        ms = [send(g.at[ia, part], g.at[ia, part], towards(b, d)) for d in (1, 2, 3)]
        yield
        for m in ms:
            m.wait_recv()
        rows, top, low = (pl.ds(aligned(base + i, half), n) for i, n in ((0, w), (0, half), (half, half)))
        right = send(g.at[ia, rows], g.at[ia, rows], towards(a, 1))
        left = send(g.at[ia, rows], g.at[ia, rows], towards(a, 3))

        def inner_part(j, start):
            bh, bl = split(g[j, rows, :])
            chunk, cols = n0 // 256, pl.ds(n0 % 256, w)
            for m in (0, 256):
                at = slice(m, m + 256)
                part = dot3(rh[j, at, :], rl[j, at, :], bh, bl, NT)
                inner[0, chunk, at, cols] = part if start else inner[0, chunk, at, cols] + part

        yield
        inner_part(ia, True)
        yield
        right.wait_recv()
        on_right = send(g.at[before, top], g.at[before, top], towards(a, 1))
        left.wait_recv()
        on_left = send(g.at[after, low], g.at[after, low], towards(a, 3))
        yield
        inner_part(before, False)
        inner_part(after, False)
        yield
        on_right.wait_recv()
        on_left.wait_recv()
        inner_part(opposite, False)

    xs, ys, zs = (1, 0, 0), (0, 1, 0), (0, 0, 1)
    orders = (
        ((other, core, 0), (0, other, core), (core, 0, other)),
        ((core, other, 0), (0, core, other), (other, 0, core)),
        (zs, xs, ys),
    )
    groups = [
        gradient(*group, *order, *(held[i] for held in (relay, ra, acc, rb, ring)))
        for i, (group, order) in enumerate(zip(GROUPS, orders))
    ]
    lockstep(groups)
    inner_sent = [send(inner.at[0, i], inner.at[1, i], partner) for i in range(2)]
    g_half = g.at[:, pl.ds(aligned(512 * core, 512), 512)]
    g_sent = send(g_half, g_half, partner)

    def image(side, i, yy):
        for m in (0, 256):
            rows = slice(m, m + 256)
            ih[rows, :], il[rows, :] = split(inner[side, i, rows, :])
        bh, bl = rank_rows(yy)
        for n in range(0, 1024, 256):
            cols = slice(n, n + 256)
            part = dot3(ih[...], il[...], bh[:, cols], bl[:, cols], NN)
            rest[:, cols] = part if (side, i) == (0, 0) else rest[:, cols] + part

    for i in range(2):
        image(0, i, 2 * core + i)
    for i in range(2):
        inner_sent[i].wait_recv()
        image(1, i, 2 * other + i)

    def fold(v):
        return functools.reduce(jnp.add, [v[:, i : i + 128] for i in range(0, v.shape[1], 128)])

    def squares(load, steps):
        def body(i, total):
            v = load(i)
            return total + jnp.sum((v * v).reshape(-1, 8, v.shape[1]), axis=0)

        return fold(lax.fori_loop(0, steps, body, jnp.zeros_like(load(0)[:8, :])))

    def share(value, slots, at, peers):
        slots[at] = value
        return [send(slots.at[at], slots.at[at], p) for p in peers]

    def gathered(messages, slots):
        for m in messages:
            m.wait_recv()
        return functools.reduce(jnp.add, [slots[i] for i in range(slots.shape[0])])

    denom = squares(lambda i: rest[pl.ds(aligned(32 * i, 32), 32), :], 16)
    messages = share(denom, slots_z, 2 * z + core, near_z)
    g_sent.wait_recv()
    numer = squares(lambda i: g[lax.div(i, 8), pl.ds(aligned(128 * lax.rem(i, 8), 128), 128), :], 32)
    messages = share(gathered(messages, slots_z), slots_xy, 4 * y + x, near_xy)
    denom = gathered(messages, slots_xy)
    total = lambda v: jnp.sum(jnp.sum(v, axis=0, keepdims=True), axis=1, keepdims=True)
    step = total(numer) / total(denom)

    def update(b, _):
        by, bx = lax.div(b, 4), lax.rem(b, 4)
        at2, at1 = by * other + bx * core, bx * other + by * core
        rows, from_rows = pl.ds(aligned(64 * b, 64), 64), pl.ds(aligned(64 * at1, 64), 64)
        for j in range(4):
            cols = slice(256 * j, 256 * j + 256)
            out[rows, cols] = z_in[at2, from_rows, cols] + step * g[j, rows, :]
        return 0

    lax.fori_loop(0, 16, update, 0)

    for copy in send.sent:
        copy.wait_send()


def scratch():
    v = pltpu.VMEM
    rows = [w for _, w in GROUPS]
    return [
        v((1024, 512), F32), v((4, 256, 1024), F32), v((4, 256, 1024), F32),
        v((4, 512, 256), F32), v((512, 1024), F32), v((4, 256, 512), F32), v((2, 256, 512), F32), v((4, 1024, 256), F32),
        v((4, 256, 1024), BF16), v((4, 256, 1024), BF16), v((4, 512, 256), BF16), v((4, 512, 256), BF16),
        v((4, 256, 1024), BF16), v((4, 256, 1024), BF16), v((4, 512, 256), BF16), v((4, 512, 256), BF16),
        v((512, 1024), BF16), v((512, 1024), BF16), v((512, 512), BF16), v((512, 512), BF16),
        v((2, 2, 512, 256), F32), v((512, 256), BF16), v((512, 256), BF16),
        v((4, 512, 256), F32), [v((2, w // 2, 256), F32) for w in rows], [v((2, w, 256), F32) for w in rows],
        [v((w, 256), F32) for w in rows], [v((3, w // 4, 256), F32) for w in rows],
        [v((4, w // 4, 256), F32) for w in rows],
        v((8, 8, 128), F32), v((16, 8, 128), F32),
        pltpu.SemaphoreType.DMA((MESSAGES,)), pltpu.SemaphoreType.DMA((MESSAGES,)), pltpu.SemaphoreType.DMA((20,)),
    ]


def shards(pair_integrals, left_factor, core, right_factor):
    in_hbm = functools.partial(pltpu.with_memory_space_constraint, memory_space=pltpu.HBM)
    return pl.pallas_call(
        kernel,
        out_shape=pltpu.VMEM((1024, 1024), F32),
        in_specs=[pl.BlockSpec(memory_space=pltpu.HBM)] * 4,
        out_specs=pl.BlockSpec(memory_space=pltpu.VMEM),
        scratch_shapes=scratch(),
        compiler_params=pltpu.CompilerParams(
            collective_id=0, has_side_effects=True, vmem_limit_bytes=54 * 1024 * 1024
        ),
        cost_estimate=pl.CostEstimate(flops=7 * 10**9, bytes_accessed=16 * 2**20, transcendentals=0),
    )(*map(in_hbm, (pair_integrals, left_factor.T, core, right_factor)))


def solution(mesh):
    placed = (P("rows", "cols"), P("rows", "cols"), P(), P("cols", "rows"))
    return jax.shard_map(shards, mesh=mesh, in_specs=placed, out_specs=P(), check_vma=False)
```

```python
import functools

import jax
import jax.numpy as jnp
from jax import lax
from jax.experimental import pallas as pl
from jax.experimental.pallas import tpu as pltpu
from jax.sharding import PartitionSpec as P

MESH = pl.DeviceIdType.MESH
F32, BF16 = jnp.float32, jnp.bfloat16
GROUPS = ((0, 128), (128, 128), (256, 128), (384, 128))
MESSAGES = 176
NN = (((1,), (0,)), ((), ()))
NT = (((1,), (1,)), ((), ()))


def split(v):
    hi = v.astype(BF16)
    return hi, (v - hi.astype(F32)).astype(BF16)


def dot3(ah, al, bh, bl, dims):
    (da,), (db,) = dims[0]
    return lax.dot_general(
        jnp.concatenate([ah, ah, al], da),
        jnp.concatenate([bh, bl, bh], db),
        dimension_numbers=dims,
        preferred_element_type=F32,
    )


def aligned(i, m):
    return pl.multiple_of(i, m)


class Sender:
    def __init__(self, send_sems, recv_sems):
        self.send_sems, self.recv_sems, self.sent = send_sems, recv_sems, []

    def __call__(self, src, dst, peer):
        i = len(self.sent)
        copy = pltpu.make_async_remote_copy(
            src_ref=src,
            dst_ref=dst,
            send_sem=self.send_sems.at[i],
            recv_sem=self.recv_sems.at[i],
            device_id=peer,
            device_id_type=MESH,
        )
        copy.start()
        self.sent.append(copy)
        return copy


def lockstep(generators):
    live = list(generators)
    while live:
        still = []
        for g in live:
            try:
                next(g)
                still.append(g)
            except StopIteration:
                pass
        live = still


def kernel(
    v_hbm, l_hbm, z_hbm, r_hbm, out,
    v_in, z_in, lt, r4, rest, u, u_in, g,
    zh, zl, rh, rl, lth, ltl, mh, ml, resh, resl, uh, ul, inner, ih, il,
    gp, relay, ra, acc, rb, ring, slots_z, slots_xy, send_sems, recv_sems, local_sems,
):
    r, c = lax.axis_index("rows"), lax.axis_index("cols")
    core, z_lo, z_hi = lax.rem(r, 2), lax.div(r, 2), lax.rem(c, 2)
    x, y, z = lax.rem(lax.div(c, 2), 4), lax.div(c, 8), 2 * z_hi + z_lo
    other = 1 - core

    def device(dx, dy, dz, k):
        xx, yy, zz = lax.rem(x + dx, 4), lax.rem(y + dy, 4), lax.rem(z + dz, 4)
        return (2 * lax.rem(zz, 2) + k, 8 * yy + 2 * xx + lax.div(zz, 2))

    partner = device(0, 0, 0, other)
    z_lo_partner = (2 * (1 - z_lo) + core, c)
    z_hi_partner = device(0, 0, 2, core)
    near_z = [device(0, 0, d, k) for d in range(4) for k in (core, other)][1:]
    near_xy = [device(dx, dy, 0, core) for dx in range(4) for dy in range(4)][1:]
    first = [device(d * other, d * core, 0, core) for d in range(4)]
    second = [device(d * core, d * other, 0, core) for d in range(4)]
    i1, i2 = x * other + y * core, y * other + x * core

    at_l = (i2, pl.ds(aligned(64 * i1 + 32 * z_hi, 32), 32))
    copy_l = pltpu.make_async_copy(l_hbm, lt.at[at_l], local_sems.at[0])
    copy_r = pltpu.make_async_copy(r_hbm, r4.at[r], local_sems.at[1])
    copy_v = pltpu.make_async_copy(v_hbm, v_in, local_sems.at[2])
    copy_l.start()
    copy_r.start()
    copy_v.start()
    copy_z = []
    for b in range(16):
        by, bx = b // 4, b % 4
        at2, at1 = by * other + bx * core, bx * other + by * core
        copy_z.append(
            pltpu.make_async_copy(
                z_hbm.at[pl.ds(64 * b, 64), :],
                z_in.at[at2, pl.ds(aligned(64 * at1, 64), 64), :],
                local_sems.at[4 + b],
            )
        )
        copy_z[-1].start()

    barrier = pltpu.get_barrier_semaphore()
    greeted = [first[1], first[3], second[1], second[3], z_hi_partner, z_lo_partner, partner]
    for other_device in greeted:
        pl.semaphore_signal(barrier, inc=1, device_id=other_device, device_id_type=MESH)
    pl.semaphore_wait(barrier, len(greeted))

    send = Sender(send_sems, recv_sems)

    def shard(d1, d2, h):
        at1, at2 = lax.rem(i1 + d1, 4), lax.rem(i2 + d2, 4)
        return lt.at[at2, pl.ds(aligned(64 * at1 + 32 * h, 32), 32), :]

    def spread(ref, peers):
        return send(ref, ref, peers[1]), send(ref, ref, peers[3])

    own, far = z_hi, 1 - z_hi
    copy_l.wait()
    mine = shard(0, 0, own)
    to_z = send(mine, mine, z_hi_partner)
    near_own = spread(mine, first)
    wide = {(0, "own"): spread(mine, second)}

    copy_r.wait()
    r_to_core = send(r4.at[r], r4.at[r], partner)
    r_to_z = send(r4.at[r], r4.at[r], z_lo_partner)

    def transpose_v(i):
        rest[:, 128 * i : 128 * i + 128] = jnp.transpose(v_in[128 * i : 128 * i + 128, :])

    copy_v.wait()
    for i in range(4):
        transpose_v(i)

    to_z.wait_recv()
    theirs = shard(0, 0, far)
    near_far = spread(theirs, first)
    wide[0, "far"] = spread(theirs, second)
    for i in range(4, 8):
        transpose_v(i)

    near_own[0].wait_recv()
    ref = shard(3, 0, own)
    through_own = send(ref, ref, first[1])
    wide[3, "own"] = spread(ref, second)
    near_own[1].wait_recv()
    wide[1, "own"] = spread(shard(1, 0, own), second)
    near_far[1].wait_recv()
    ref = shard(1, 0, far)
    through_far = send(ref, ref, first[3])
    wide[1, "far"] = spread(ref, second)
    near_far[0].wait_recv()
    wide[3, "far"] = spread(shard(3, 0, far), second)

    passed = []

    def pass_on(d1):
        wide[d1, "own"][0].wait_recv()
        ref = shard(d1, 3, own)
        passed.append(send(ref, ref, second[1]))
        wide[d1, "far"][1].wait_recv()
        ref = shard(d1, 1, far)
        passed.append(send(ref, ref, second[3]))

    pass_on(0)
    through_own.wait_recv()
    wide[2, "own"] = spread(shard(2, 0, own), second)
    through_far.wait_recv()
    wide[2, "far"] = spread(shard(2, 0, far), second)

    for copy in copy_z:
        copy.wait()

    def split_z(i, _):
        zh[i], zl[i] = split(z_in[i])
        return 0

    lax.fori_loop(0, 4, split_z, 0)
    pass_on(3)
    pass_on(1)

    r_to_z.wait_recv()
    r_far = r4.at[2 * (1 - z_lo) + core]
    r_on = send(r_far, r_far, partner)
    r_to_core.wait_recv()
    r_on.wait_recv()

    def split_r(i, _):
        rh[i], rl[i] = split(r4[i])
        return 0

    lax.fori_loop(0, 4, split_r, 0)

    def mix(i, _):
        for m in (0, 256):
            rows = slice(m, m + 256)
            ah, al = (jnp.concatenate([ref[k, rows, :] for k in range(4)], 1) for ref in (rh, rl))
            mh[i, rows, :], ml[i, rows, :] = split(dot3(ah, al, zh[i], zl[i], NT))
        return 0

    mix(i2, 0)
    mix(lax.rem(i2 + 3, 4), 0)

    def subtract(i):
        lth[i], ltl[i] = split(lt[i])
        for n in range(0, 1024, 256):
            cols = slice(n, n + 256)
            rest[:, cols] -= dot3(mh[i], ml[i], lth[i, :, cols], ltl[i, :, cols], NN)

    pass_on(2)
    mix(lax.rem(i2 + 1, 4), 0)
    mix(lax.rem(i2 + 2, 4), 0)
    subtract(i2)
    for d1 in range(4):
        wide[d1, "far"][0].wait_recv()
    subtract(lax.rem(i2 + 3, 4))
    for d1 in range(4):
        wide[d1, "own"][1].wait_recv()
    subtract(lax.rem(i2 + 1, 4))
    for copy in passed:
        copy.wait_recv()
    subtract(lax.rem(i2 + 2, 4))

    def split_rest(i, _):
        rows = pl.ds(aligned(128 * i, 128), 128)
        resh[rows, :], resl[rows, :] = split(rest[rows, :])
        return 0

    lax.fori_loop(0, 4, split_rest, 0)

    def rank_rows(yy):
        parts = []
        for j in range(4):
            at2, at1 = yy * other + j * core, j * other + yy * core
            rows = pl.ds(aligned(64 * at1, 64), 64)
            parts.append((lth[at2, rows, :], ltl[at2, rows, :]))
        return (jnp.concatenate([p[i] for p in parts], axis=0) for i in (0, 1))

    def project(yy):
        ah, al = rank_rows(yy)
        u[yy] = dot3(ah, al, resh[...], resl[...], NT)

    def take(j):
        rows = slice(256 * j, 256 * j + 256)
        u_sent[j].wait_recv()
        uh[rows, :], ul[rows, :] = split(u[2 * core + j] + u_in[j])

    u_sent = []
    for j in range(2):
        project(2 * other + j)
        u_sent.append(send(u.at[2 * other + j], u_in.at[j], partner))
    def gradient(n0, w, a, b, e, relay, ra, acc, rb, ring):
        half = w // 2
        ia, ib, ie = (x * v[0] + y * v[1] + z * v[2] for v in (a, b, e))
        towards = lambda v, d: device(d * v[0], d * v[1], d * v[2], core)
        opposite, after, before = (lax.rem(ia + d, 4) for d in (2, 1, 3))
        rows, top, low = pl.ds(n0, w), pl.ds(n0, half), pl.ds(n0 + half, half)

        def term(j):
            gp[j, rows, :] = dot3(uh[rows, :], ul[rows, :], rh[j], rl[j], NN)

        term(opposite)
        m1 = send(gp.at[opposite, top], relay.at[0], towards(a, 1))
        m2 = send(gp.at[opposite, low], relay.at[1], towards(a, 3))
        yield
        term(after)
        m3 = send(gp.at[after, low], ra.at[0, pl.ds(half, half)], towards(a, 1))
        term(before)
        m4 = send(gp.at[before, top], ra.at[1, pl.ds(0, half)], towards(a, 3))
        yield
        m1.wait_recv()
        gp[after, top, :] += relay[0]
        m5 = send(gp.at[after, top], ra.at[0, pl.ds(0, half)], towards(a, 1))
        m2.wait_recv()
        gp[before, low, :] += relay[1]
        m6 = send(gp.at[before, low], ra.at[1, pl.ds(half, half)], towards(a, 3))
        yield
        term(ia)
        yield
        for m in (m3, m4, m5, m6):
            m.wait_recv()
        acc[...] = gp[ia, rows, :] + ra[0] + ra[1]
        quarter = w // 4
        ms = []
        for d in (1, 2, 3):
            part = pl.ds(aligned(quarter * lax.rem(ib + d, 4), quarter), quarter)
            ms.append(send(acc.at[part], rb.at[d - 1], towards(b, d)))
        yield
        for m in ms:
            m.wait_recv()
        ring[ie] = acc[pl.ds(aligned(quarter * ib, quarter), quarter), :] + rb[0] + rb[1] + rb[2]
        ms = [send(ring.at[ie], ring.at[ie], towards(e, d)) for d in (1, 2, 3)]
        yield
        for m in ms:
            m.wait_recv()
        base = 512 * core + n0
        part = pl.ds(aligned(base + quarter * ib, quarter), quarter)
        g[ia, part, :] = ring[0] + ring[1] + ring[2] + ring[3]
        ms = [send(g.at[ia, part], g.at[ia, part], towards(b, d)) for d in (1, 2, 3)]
        yield
        for m in ms:
            m.wait_recv()
        rows, top, low = (pl.ds(aligned(base + i, half), n) for i, n in ((0, w), (0, half), (half, half)))
        right = send(g.at[ia, rows], g.at[ia, rows], towards(a, 1))
        left = send(g.at[ia, rows], g.at[ia, rows], towards(a, 3))

        def inner_part(j, start):
            bh, bl = split(g[j, rows, :])
            chunk, cols = n0 // 256, pl.ds(n0 % 256, w)
            for m in (0, 256):
                at = slice(m, m + 256)
                part = dot3(rh[j, at, :], rl[j, at, :], bh, bl, NT)
                inner[0, chunk, at, cols] = part if start else inner[0, chunk, at, cols] + part

        yield
        inner_part(ia, True)
        yield
        right.wait_recv()
        on_right = send(g.at[before, top], g.at[before, top], towards(a, 1))
        left.wait_recv()
        on_left = send(g.at[after, low], g.at[after, low], towards(a, 3))
        yield
        inner_part(before, False)
        inner_part(after, False)
        yield
        on_right.wait_recv()
        on_left.wait_recv()
        inner_part(opposite, False)

    xs, ys, zs = (1, 0, 0), (0, 1, 0), (0, 0, 1)
    orders = (
        ((other, core, 0), (0, other, core), (core, 0, other)),
        ((other, core, 0), (0, other, core), (core, 0, other)),
        ((core, other, 0), (0, core, other), (other, 0, core)),
        (zs, xs, ys),
    )
    groups = [
        gradient(*group, *order, *(held[i] for held in (relay, ra, acc, rb, ring)))
        for i, (group, order) in enumerate(zip(GROUPS, orders))
    ]
    project(2 * core)
    take(0)
    for steps in groups[:2]:
        next(steps)
    project(2 * core + 1)
    for steps in groups[:2]:
        next(steps)
    take(1)
    for steps in groups[2:] * 2:
        next(steps)
    lockstep(groups)
    inner_sent = [send(inner.at[0, i], inner.at[1, i], partner) for i in range(2)]
    g_half = g.at[:, pl.ds(aligned(512 * core, 512), 512)]
    g_sent = send(g_half, g_half, partner)

    def image(side, i, yy):
        for m in (0, 256):
            rows = slice(m, m + 256)
            ih[rows, :], il[rows, :] = split(inner[side, i, rows, :])
        bh, bl = rank_rows(yy)
        for n in range(0, 1024, 256):
            cols = slice(n, n + 256)
            part = dot3(ih[...], il[...], bh[:, cols], bl[:, cols], NN)
            rest[:, cols] = part if (side, i) == (0, 0) else rest[:, cols] + part

    for i in range(2):
        image(0, i, 2 * core + i)
    for i in range(2):
        inner_sent[i].wait_recv()
        image(1, i, 2 * other + i)

    def fold(v):
        return functools.reduce(jnp.add, [v[:, i : i + 128] for i in range(0, v.shape[1], 128)])

    def squares(load, steps):
        def body(i, total):
            v = load(i)
            return total + jnp.sum((v * v).reshape(-1, 8, v.shape[1]), axis=0)

        return fold(lax.fori_loop(0, steps, body, jnp.zeros_like(load(0)[:8, :])))

    def share(value, slots, at, peers):
        slots[at] = value
        return [send(slots.at[at], slots.at[at], p) for p in peers]

    def gathered(messages, slots):
        for m in messages:
            m.wait_recv()
        return functools.reduce(jnp.add, [slots[i] for i in range(slots.shape[0])])

    denom = squares(lambda i: rest[pl.ds(aligned(32 * i, 32), 32), :], 16)
    messages = share(denom, slots_z, 2 * z + core, near_z)
    g_sent.wait_recv()
    numer = squares(lambda i: g[lax.div(i, 8), pl.ds(aligned(128 * lax.rem(i, 8), 128), 128), :], 32)
    messages = share(gathered(messages, slots_z), slots_xy, 4 * y + x, near_xy)
    denom = gathered(messages, slots_xy)
    total = lambda v: jnp.sum(jnp.sum(v, axis=0, keepdims=True), axis=1, keepdims=True)
    step = total(numer) / total(denom)

    def update(b, _):
        by, bx = lax.div(b, 4), lax.rem(b, 4)
        at2, at1 = by * other + bx * core, bx * other + by * core
        rows, from_rows = pl.ds(aligned(64 * b, 64), 64), pl.ds(aligned(64 * at1, 64), 64)
        for j in range(4):
            cols = slice(256 * j, 256 * j + 256)
            out[rows, cols] = z_in[at2, from_rows, cols] + step * g[j, rows, :]
        return 0

    lax.fori_loop(0, 16, update, 0)

    for copy in send.sent:
        copy.wait_send()


def scratch():
    v = pltpu.VMEM
    rows = [w for _, w in GROUPS]
    return [
        v((1024, 512), F32), v((4, 256, 1024), F32), v((4, 256, 1024), F32),
        v((4, 512, 256), F32), v((512, 1024), F32), v((4, 256, 512), F32), v((2, 256, 512), F32), v((4, 1024, 256), F32),
        v((4, 256, 1024), BF16), v((4, 256, 1024), BF16), v((4, 512, 256), BF16), v((4, 512, 256), BF16),
        v((4, 256, 1024), BF16), v((4, 256, 1024), BF16), v((4, 512, 256), BF16), v((4, 512, 256), BF16),
        v((512, 1024), BF16), v((512, 1024), BF16), v((512, 512), BF16), v((512, 512), BF16),
        v((2, 2, 512, 256), F32), v((512, 256), BF16), v((512, 256), BF16),
        v((4, 512, 256), F32), [v((2, w // 2, 256), F32) for w in rows], [v((2, w, 256), F32) for w in rows],
        [v((w, 256), F32) for w in rows], [v((3, w // 4, 256), F32) for w in rows],
        [v((4, w // 4, 256), F32) for w in rows],
        v((8, 8, 128), F32), v((16, 8, 128), F32),
        pltpu.SemaphoreType.DMA((MESSAGES,)), pltpu.SemaphoreType.DMA((MESSAGES,)), pltpu.SemaphoreType.DMA((20,)),
    ]


def shards(pair_integrals, left_factor, core, right_factor):
    in_hbm = functools.partial(pltpu.with_memory_space_constraint, memory_space=pltpu.HBM)
    return pl.pallas_call(
        kernel,
        out_shape=pltpu.VMEM((1024, 1024), F32),
        in_specs=[pl.BlockSpec(memory_space=pltpu.HBM)] * 4,
        out_specs=pl.BlockSpec(memory_space=pltpu.VMEM),
        scratch_shapes=scratch(),
        compiler_params=pltpu.CompilerParams(
            collective_id=0, has_side_effects=True, vmem_limit_bytes=54 * 1024 * 1024
        ),
        cost_estimate=pl.CostEstimate(flops=7 * 10**9, bytes_accessed=16 * 2**20, transcendentals=0),
    )(*map(in_hbm, (pair_integrals, left_factor.T, core, right_factor)))


def solution(mesh):
    placed = (P("rows", "cols"), P("rows", "cols"), P(), P("cols", "rows"))
    return jax.shard_map(shards, mesh=mesh, in_specs=placed, out_specs=P(), check_vma=False)
```

```python
import functools

import jax
import jax.numpy as jnp
from jax import lax
from jax.experimental import pallas as pl
from jax.experimental.pallas import tpu as pltpu
from jax.sharding import PartitionSpec as P

MESH = pl.DeviceIdType.MESH
F32, BF16 = jnp.float32, jnp.bfloat16
GROUPS = ((0, 128), (128, 128), (256, 128), (384, 128))
MESSAGES = 176
NN = (((1,), (0,)), ((), ()))
NT = (((1,), (1,)), ((), ()))


def split(v):
    hi = v.astype(BF16)
    return hi, (v - hi.astype(F32)).astype(BF16)


def dot3(ah, al, bh, bl, dims):
    (da,), (db,) = dims[0]
    return lax.dot_general(
        jnp.concatenate([ah, ah, al], da),
        jnp.concatenate([bh, bl, bh], db),
        dimension_numbers=dims,
        preferred_element_type=F32,
    )


def aligned(i, m):
    return pl.multiple_of(i, m)


class Sender:
    def __init__(self, send_sems, recv_sems):
        self.send_sems, self.recv_sems, self.sent = send_sems, recv_sems, []

    def __call__(self, src, dst, peer):
        i = len(self.sent)
        copy = pltpu.make_async_remote_copy(
            src_ref=src,
            dst_ref=dst,
            send_sem=self.send_sems.at[i],
            recv_sem=self.recv_sems.at[i],
            device_id=peer,
            device_id_type=MESH,
        )
        copy.start()
        self.sent.append(copy)
        return copy


def lockstep(generators):
    live = list(generators)
    while live:
        still = []
        for g in live:
            try:
                next(g)
                still.append(g)
            except StopIteration:
                pass
        live = still


def kernel(
    v_hbm, l_hbm, z_hbm, r_hbm, out,
    v_in, z_in, lt, r4, rest, u, u_in, g,
    zh, zl, rh, rl, lth, ltl, mixed, mh, ml, resh, resl, uh, ul, inner, ih, il,
    gp, relay, ra, acc, rb, ring, slots_z, slots_xy, send_sems, recv_sems, local_sems,
):
    r, c = lax.axis_index("rows"), lax.axis_index("cols")
    core, z_lo, z_hi = lax.rem(r, 2), lax.div(r, 2), lax.rem(c, 2)
    x, y, z = lax.rem(lax.div(c, 2), 4), lax.div(c, 8), 2 * z_hi + z_lo
    other = 1 - core

    def device(dx, dy, dz, k):
        xx, yy, zz = lax.rem(x + dx, 4), lax.rem(y + dy, 4), lax.rem(z + dz, 4)
        return (2 * lax.rem(zz, 2) + k, 8 * yy + 2 * xx + lax.div(zz, 2))

    partner = device(0, 0, 0, other)
    z_lo_partner = (2 * (1 - z_lo) + core, c)
    z_hi_partner = device(0, 0, 2, core)
    near_z = [device(0, 0, d, k) for d in range(4) for k in (core, other)][1:]
    near_xy = [device(dx, dy, 0, core) for dx in range(4) for dy in range(4)][1:]
    first = [device(d * other, d * core, 0, core) for d in range(4)]
    second = [device(d * core, d * other, 0, core) for d in range(4)]
    i1, i2 = x * other + y * core, y * other + x * core

    barrier = pltpu.get_barrier_semaphore()
    greeted = [*first[1:], second[1], second[3], z_hi_partner, z_lo_partner, partner]
    for other_device in greeted:
        pl.semaphore_signal(barrier, inc=1, device_id=other_device, device_id_type=MESH)
    at_l = (i2, pl.ds(aligned(64 * i1 + 32 * z_hi, 32), 32))
    copy_l = pltpu.make_async_copy(l_hbm, lt.at[at_l], local_sems.at[0])
    copy_r = pltpu.make_async_copy(r_hbm, r4.at[r], local_sems.at[1])
    copy_v = pltpu.make_async_copy(v_hbm, v_in, local_sems.at[2])
    copy_l.start()
    copy_r.start()
    copy_v.start()
    copy_z = []
    for b in range(16):
        by, bx = b // 4, b % 4
        at2, at1 = by * other + bx * core, bx * other + by * core
        copy_z.append(
            pltpu.make_async_copy(
                z_hbm.at[pl.ds(64 * b, 64), :],
                z_in.at[at2, pl.ds(aligned(64 * at1, 64), 64), :],
                local_sems.at[4 + b],
            )
        )
        copy_z[-1].start()

    def transpose_v(i):
        rest[:, 128 * i : 128 * i + 128] = jnp.transpose(v_in[128 * i : 128 * i + 128, :])

    copy_v.wait()
    for i in range(8):
        transpose_v(i)
    pl.semaphore_wait(barrier, len(greeted))

    send = Sender(send_sems, recv_sems)

    def shard(d1, d2, h):
        at1, at2 = lax.rem(i1 + d1, 4), lax.rem(i2 + d2, 4)
        return lt.at[at2, pl.ds(aligned(64 * at1 + 32 * h, 32), 32), :]

    def spread(ref, peers):
        return send(ref, ref, peers[1]), send(ref, ref, peers[3])

    own, far = z_hi, 1 - z_hi
    copy_l.wait()
    mine = shard(0, 0, own)
    to_z = send(mine, mine, z_hi_partner)
    near_own = spread(mine, first)
    through_own = send(mine, mine, first[2])
    wide = {(0, "own"): spread(mine, second)}

    copy_r.wait()
    r_to_core = send(r4.at[r], r4.at[r], partner)

    def split_z(i, _):
        zh[i], zl[i] = split(z_in[i])
        return 0

    for copy in copy_z:
        copy.wait()
    lax.fori_loop(0, 4, split_z, 0)
    to_z.wait_recv()
    r_to_z = send(r4.at[r], r4.at[r], z_lo_partner)
    theirs = shard(0, 0, far)
    near_far = spread(theirs, first)
    through_far = send(theirs, theirs, first[2])
    wide[0, "far"] = spread(theirs, second)
    near_own[0].wait_recv()
    ref = shard(3, 0, own)
    wide[3, "own"] = spread(ref, second)
    near_own[1].wait_recv()
    wide[1, "own"] = spread(shard(1, 0, own), second)
    near_far[1].wait_recv()
    ref = shard(1, 0, far)
    wide[1, "far"] = spread(ref, second)
    near_far[0].wait_recv()
    wide[3, "far"] = spread(shard(3, 0, far), second)

    passed = []

    def pass_on(d1):
        wide[d1, "own"][0].wait_recv()
        ref = shard(d1, 3, own)
        passed.append(send(ref, ref, second[1]))
        wide[d1, "far"][1].wait_recv()
        ref = shard(d1, 1, far)
        passed.append(send(ref, ref, second[3]))

    def split_r(k):
        rh[k], rl[k] = split(r4[k])

    def mix(i, chip):
        k = pl.ds(aligned(512 * chip, 512), 512)
        for m in (0, 256):
            rows = slice(m, m + 256)
            ah, al = (jnp.concatenate([ref[2 * chip + j, rows, :] for j in (0, 1)], 1) for ref in (rh, rl))
            yield rows, dot3(ah, al, zh[i, :, k], zl[i, :, k], NT)

    def mix_first(i):
        for rows, part in mix(i, z_lo):
            mixed[i, rows, :] = part

    def mix_rest(i):
        for rows, part in mix(i, 1 - z_lo):
            mh[i, rows, :], ml[i, rows, :] = split(mixed[i, rows, :] + part)

    through_own.wait_recv()
    wide[2, "own"] = spread(shard(2, 0, own), second)
    pass_on(0)
    through_far.wait_recv()
    wide[2, "far"] = spread(shard(2, 0, far), second)

    split_r(r)
    r_to_core.wait_recv()
    split_r(2 * z_lo + other)
    mix_first(0)
    pass_on(3)
    mix_first(1)
    pass_on(1)
    mix_first(2)
    mix_first(3)

    r_to_z.wait_recv()
    r_far = r4.at[2 * (1 - z_lo) + core]
    r_on = send(r_far, r_far, partner)
    split_r(2 * (1 - z_lo) + core)
    pass_on(2)
    r_on.wait_recv()
    split_r(2 * (1 - z_lo) + other)

    def subtract(i):
        lth[i], ltl[i] = split(lt[i])
        for n in range(0, 1024, 256):
            cols = slice(n, n + 256)
            rest[:, cols] -= dot3(mh[i], ml[i], lth[i, :, cols], ltl[i, :, cols], NN)

    mix_rest(i2)
    subtract(i2)
    mix_rest(lax.rem(i2 + 3, 4))
    for d1 in range(4):
        wide[d1, "far"][0].wait_recv()
    subtract(lax.rem(i2 + 3, 4))
    mix_rest(lax.rem(i2 + 1, 4))
    for d1 in range(4):
        wide[d1, "own"][1].wait_recv()
    subtract(lax.rem(i2 + 1, 4))
    mix_rest(lax.rem(i2 + 2, 4))
    for copy in passed:
        copy.wait_recv()
    subtract(lax.rem(i2 + 2, 4))

    def split_rest(i, _):
        rows = pl.ds(aligned(128 * i, 128), 128)
        resh[rows, :], resl[rows, :] = split(rest[rows, :])
        return 0

    lax.fori_loop(0, 4, split_rest, 0)

    def rank_rows(yy):
        parts = []
        for j in range(4):
            at2, at1 = yy * other + j * core, j * other + yy * core
            rows = pl.ds(aligned(64 * at1, 64), 64)
            parts.append((lth[at2, rows, :], ltl[at2, rows, :]))
        return (jnp.concatenate([p[i] for p in parts], axis=0) for i in (0, 1))

    def project(yy):
        ah, al = rank_rows(yy)
        u[yy] = dot3(ah, al, resh[...], resl[...], NT)

    def take(j):
        rows = slice(256 * j, 256 * j + 256)
        u_sent[j].wait_recv()
        uh[rows, :], ul[rows, :] = split(u[2 * core + j] + u_in[j])

    u_sent = []
    for j in range(2):
        project(2 * other + j)
        u_sent.append(send(u.at[2 * other + j], u_in.at[j], partner))
    def gradient(n0, w, a, b, e, relay, ra, acc, rb, ring):
        half = w // 2
        ia, ib, ie = (x * v[0] + y * v[1] + z * v[2] for v in (a, b, e))
        towards = lambda v, d: device(d * v[0], d * v[1], d * v[2], core)
        opposite, after, before = (lax.rem(ia + d, 4) for d in (2, 1, 3))
        rows, top, low = pl.ds(n0, w), pl.ds(n0, half), pl.ds(n0 + half, half)

        def term(j):
            gp[j, rows, :] = dot3(uh[rows, :], ul[rows, :], rh[j], rl[j], NN)

        term(opposite)
        m1 = send(gp.at[opposite, top], relay.at[0], towards(a, 1))
        m2 = send(gp.at[opposite, low], relay.at[1], towards(a, 3))
        yield
        term(after)
        m3 = send(gp.at[after, low], ra.at[0, pl.ds(half, half)], towards(a, 1))
        term(before)
        m4 = send(gp.at[before, top], ra.at[1, pl.ds(0, half)], towards(a, 3))
        yield
        m1.wait_recv()
        gp[after, top, :] += relay[0]
        m5 = send(gp.at[after, top], ra.at[0, pl.ds(0, half)], towards(a, 1))
        m2.wait_recv()
        gp[before, low, :] += relay[1]
        m6 = send(gp.at[before, low], ra.at[1, pl.ds(half, half)], towards(a, 3))
        yield
        term(ia)
        yield
        for m in (m3, m4, m5, m6):
            m.wait_recv()
        acc[...] = gp[ia, rows, :] + ra[0] + ra[1]
        quarter = w // 4
        ms = []
        for d in (1, 2, 3):
            part = pl.ds(aligned(quarter * lax.rem(ib + d, 4), quarter), quarter)
            ms.append(send(acc.at[part], rb.at[d - 1], towards(b, d)))
        yield
        for m in ms:
            m.wait_recv()
        ring[ie] = acc[pl.ds(aligned(quarter * ib, quarter), quarter), :] + rb[0] + rb[1] + rb[2]
        ms = [send(ring.at[ie], ring.at[ie], towards(e, d)) for d in (1, 2, 3)]
        yield
        for m in ms:
            m.wait_recv()
        base = 512 * core + n0
        part = pl.ds(aligned(base + quarter * ib, quarter), quarter)
        g[ia, part, :] = ring[0] + ring[1] + ring[2] + ring[3]
        ms = [send(g.at[ia, part], g.at[ia, part], towards(b, d)) for d in (1, 2, 3)]
        yield
        for m in ms:
            m.wait_recv()
        rows, top, low = (pl.ds(aligned(base + i, half), n) for i, n in ((0, w), (0, half), (half, half)))
        right = send(g.at[ia, rows], g.at[ia, rows], towards(a, 1))
        left = send(g.at[ia, rows], g.at[ia, rows], towards(a, 3))

        def inner_part(j, start):
            bh, bl = split(g[j, rows, :])
            chunk, cols = n0 // 256, pl.ds(n0 % 256, w)
            for m in (0, 256):
                at = slice(m, m + 256)
                part = dot3(rh[j, at, :], rl[j, at, :], bh, bl, NT)
                inner[0, chunk, at, cols] = part if start else inner[0, chunk, at, cols] + part

        yield
        inner_part(ia, True)
        yield
        right.wait_recv()
        on_right = send(g.at[before, top], g.at[before, top], towards(a, 1))
        left.wait_recv()
        on_left = send(g.at[after, low], g.at[after, low], towards(a, 3))
        yield
        inner_part(before, False)
        inner_part(after, False)
        yield
        on_right.wait_recv()
        on_left.wait_recv()
        inner_part(opposite, False)

    xs, ys, zs = (1, 0, 0), (0, 1, 0), (0, 0, 1)
    orders = (
        ((other, core, 0), (0, other, core), (core, 0, other)),
        ((other, core, 0), (0, other, core), (core, 0, other)),
        ((core, other, 0), (0, core, other), (other, 0, core)),
        (zs, xs, ys),
    )
    groups = [
        gradient(*group, *order, *(held[i] for held in (relay, ra, acc, rb, ring)))
        for i, (group, order) in enumerate(zip(GROUPS, orders))
    ]
    project(2 * core)
    take(0)
    for steps in groups[:2]:
        next(steps)
    project(2 * core + 1)
    for steps in groups[:2]:
        next(steps)
    take(1)
    for steps in groups[2:] * 2:
        next(steps)
    lockstep(groups)
    inner_sent = [send(inner.at[0, i], inner.at[1, i], partner) for i in range(2)]
    g_half = g.at[:, pl.ds(aligned(512 * core, 512), 512)]
    g_sent = send(g_half, g_half, partner)

    def image(side, i, yy):
        for m in (0, 256):
            rows = slice(m, m + 256)
            ih[rows, :], il[rows, :] = split(inner[side, i, rows, :])
        bh, bl = rank_rows(yy)
        for n in range(0, 1024, 256):
            cols = slice(n, n + 256)
            part = dot3(ih[...], il[...], bh[:, cols], bl[:, cols], NN)
            rest[:, cols] = part if (side, i) == (0, 0) else rest[:, cols] + part

    for i in range(2):
        image(0, i, 2 * core + i)
    for i in range(2):
        inner_sent[i].wait_recv()
        image(1, i, 2 * other + i)

    def fold(v):
        return functools.reduce(jnp.add, [v[:, i : i + 128] for i in range(0, v.shape[1], 128)])

    def squares(load, steps):
        def body(i, total):
            v = load(i)
            return total + jnp.sum((v * v).reshape(-1, 8, v.shape[1]), axis=0)

        return fold(lax.fori_loop(0, steps, body, jnp.zeros_like(load(0)[:8, :])))

    def share(value, slots, at, peers):
        slots[at] = value
        return [send(slots.at[at], slots.at[at], p) for p in peers]

    def gathered(messages, slots):
        for m in messages:
            m.wait_recv()
        return functools.reduce(jnp.add, [slots[i] for i in range(slots.shape[0])])

    denom = squares(lambda i: rest[pl.ds(aligned(32 * i, 32), 32), :], 16)
    messages = share(denom, slots_z, 2 * z + core, near_z)
    g_sent.wait_recv()
    numer = squares(lambda i: g[lax.div(i, 8), pl.ds(aligned(128 * lax.rem(i, 8), 128), 128), :], 32)
    messages = share(gathered(messages, slots_z), slots_xy, 4 * y + x, near_xy)
    denom = gathered(messages, slots_xy)
    total = lambda v: jnp.sum(jnp.sum(v, axis=0, keepdims=True), axis=1, keepdims=True)
    step = total(numer) / total(denom)

    def update(b, _):
        by, bx = lax.div(b, 4), lax.rem(b, 4)
        at2, at1 = by * other + bx * core, bx * other + by * core
        rows, from_rows = pl.ds(aligned(64 * b, 64), 64), pl.ds(aligned(64 * at1, 64), 64)
        for j in range(4):
            cols = slice(256 * j, 256 * j + 256)
            out[rows, cols] = z_in[at2, from_rows, cols] + step * g[j, rows, :]
        return 0

    lax.fori_loop(0, 16, update, 0)

    for copy in send.sent:
        copy.wait_send()


def scratch():
    v = pltpu.VMEM
    rows = [w for _, w in GROUPS]
    return [
        v((1024, 512), F32), v((4, 256, 1024), F32), v((4, 256, 1024), F32),
        v((4, 512, 256), F32), v((512, 1024), F32), v((4, 256, 512), F32), v((2, 256, 512), F32), v((4, 1024, 256), F32),
        v((4, 256, 1024), BF16), v((4, 256, 1024), BF16), v((4, 512, 256), BF16), v((4, 512, 256), BF16),
        v((4, 256, 1024), BF16), v((4, 256, 1024), BF16),
        v((4, 512, 256), F32), v((4, 512, 256), BF16), v((4, 512, 256), BF16),
        v((512, 1024), BF16), v((512, 1024), BF16), v((512, 512), BF16), v((512, 512), BF16),
        v((2, 2, 512, 256), F32), v((512, 256), BF16), v((512, 256), BF16),
        v((4, 512, 256), F32), [v((2, w // 2, 256), F32) for w in rows], [v((2, w, 256), F32) for w in rows],
        [v((w, 256), F32) for w in rows], [v((3, w // 4, 256), F32) for w in rows],
        [v((4, w // 4, 256), F32) for w in rows],
        v((8, 8, 128), F32), v((16, 8, 128), F32),
        pltpu.SemaphoreType.DMA((MESSAGES,)), pltpu.SemaphoreType.DMA((MESSAGES,)), pltpu.SemaphoreType.DMA((20,)),
    ]


def shards(pair_integrals, left_factor, core, right_factor):
    in_hbm = functools.partial(pltpu.with_memory_space_constraint, memory_space=pltpu.HBM)
    return pl.pallas_call(
        kernel,
        out_shape=pltpu.VMEM((1024, 1024), F32),
        in_specs=[pl.BlockSpec(memory_space=pltpu.HBM)] * 4,
        out_specs=pl.BlockSpec(memory_space=pltpu.VMEM),
        scratch_shapes=scratch(),
        compiler_params=pltpu.CompilerParams(
            collective_id=0, has_side_effects=True, vmem_limit_bytes=54 * 1024 * 1024
        ),
        cost_estimate=pl.CostEstimate(flops=7 * 10**9, bytes_accessed=16 * 2**20, transcendentals=0),
    )(*map(in_hbm, (pair_integrals, left_factor.T, core, right_factor)))


def solution(mesh):
    placed = (P("rows", "cols"), P("rows", "cols"), P(), P("cols", "rows"))
    return jax.shard_map(shards, mesh=mesh, in_specs=placed, out_specs=P(), check_vma=False)
```
